32 devices in a mesh: dp: 4 (over y, core), sy: 4 (over z), sx: 2 (over x).
Axes of the slice: x: 2, y: 2, z: 4, core: 2. Of those that a mesh axis runs over, the one named last changes fastest.
Arguments:
- inputs: bfloat16 [4, 8, 32, 4, 512], P('dp', None, 'sy', 'sx'), may hold values from -6 to 6
- pre_activation: bfloat16 [4, 8, 32, 4, 512], P('dp', None, 'sy', 'sx'), may hold values from -6 to 6
- upstream: bfloat16 [4, 8, 32, 4, 512], P('dp', None, 'sy', 'sx'), may hold values from -6 to 6
- weight: bfloat16 [27, 512, 512], P(None, 'dp'), may hold values from -0.0546875 to 0.0546875
- first_moment: float32 [13824, 128], P(('dp', 'sy', 'sx')), may hold values from -4 to 4
- second_moment: float32 [13824, 128], P(('dp', 'sy', 'sx')), may hold values from 0.05 to 1
- hash_seed: int32 [], replicated, may hold values from 0 to 999999
- step_count: int32 [], replicated, may hold values from 1 to 29
Outputs:
- input_grad: bfloat16 [4, 8, 32, 4, 512], P('dp', None, 'sy', 'sx')
- new_first: float32 [13824, 128], P(('dp', 'sy', 'sx'))
- new_second: float32 [13824, 128], P(('dp', 'sy', 'sx'))
- scales: float32 [13824], P(('dp', 'sy', 'sx'))
The draws below stay inside these ranges and needn't reach their ends.
All inputs are finite; a program needn't handle non-finite values.
Results may differ from the reference program's by a relative error of at most 0.004.
Values may be sent and summed in bfloat16 or wider, within the bound.
A program may use at most 128 MiB of HBM per device.

```python
import math
import jax
import jax.numpy as jnp
from jax import lax

IN_CHANNELS = 512
OUT_CHANNELS = 512
LOW_RANK = 128
FRAMES = 8
SAMPLES = 4
HEIGHT = 32
WIDTH = 4
TOKENS = 4096
GRAD_ROWS = 13824


def raised(result, rng, source, target, blocks, factor):
    owner, partner = [(jnp.arange(result.shape[position]) // (result.shape[position] // blocks)).reshape([-1 if axis == position else 1 for axis in range(result.ndim)]) for position in (source, target)]
    chosen = jax.random.permutation(rng, blocks)[partner]
    strong = (owner == chosen) | (owner == (partner + blocks // 2) % blocks)
    return jnp.where(strong, factor * result, result)


def block_scale(rng, dims, shards, smallest, high):
    loudness, own = 1.0, jax.random.fold_in(rng, 6)
    for position, parts in shards:
        draws = jnp.exp(jax.random.uniform(jax.random.fold_in(own, position), (parts,), jnp.float32, smallest / len(shards), high / len(shards)))
        loudness = loudness * jnp.repeat(draws, dims[position] // parts).reshape([-1 if axis == position else 1 for axis in range(len(dims))])
    return loudness


def bell_draw(own_key, extent, width, reach, split=(), held_as=jnp.bfloat16):
    result = jax.random.normal(own_key, extent, jnp.float32) * width
    if len(split) > 0:
        result = block_scale(own_key, extent, split, -0.22, 0.18) * result
    return jnp.clip(result, min=-reach, max=reach).astype(held_as)


def bell_draw_with(key, dims, deviation, bound, cuts, heavy, held_as=jnp.bfloat16):
    entries = deviation * jax.random.normal(key, dims, jnp.float32)
    if cuts:
        entries = entries * block_scale(key, dims, cuts, -0.22, 0.18)
    return jnp.clip(raised(entries, jax.random.fold_in(key, 3), *heavy), -bound, bound).astype(held_as)


def setup_inputs(seed: int = 0) -> dict:
    seeds = jax.random.split(jax.random.key(seed), 9)
    return {
        "inputs": bell_draw_with(seeds[0], (SAMPLES, FRAMES, HEIGHT, WIDTH, IN_CHANNELS), 1.0, 6.0, ((0, 4), (2, 4), (3, 2)), (3, 4, 2, 2.0)),
        "pre_activation": bell_draw(seeds[1], (SAMPLES, FRAMES, HEIGHT, WIDTH, OUT_CHANNELS), 1.5, 6.0, ((0, 4), (2, 4), (3, 2))),
        "upstream": bell_draw(seeds[2], (SAMPLES, FRAMES, HEIGHT, WIDTH, OUT_CHANNELS), 1.0, 6.0, ((0, 4), (2, 4), (3, 2))),
        "weight": bell_draw(seeds[3], (27, IN_CHANNELS, OUT_CHANNELS), (27 * IN_CHANNELS) ** -0.5, 0.0546875, ((1, 4),)),
        "first_moment": bell_draw(seeds[4], (GRAD_ROWS, LOW_RANK), 0.5, 4.0, ((0, 32),), jnp.float32),
        "second_moment": jnp.clip(jnp.exp(math.log(1.0) - 2.9957323 * jax.random.uniform(seeds[5], (GRAD_ROWS, LOW_RANK), jnp.float32) ** block_scale(seeds[5], (GRAD_ROWS, LOW_RANK), ((0, 32),), -0.2, 0.2)), 0.05, 1.0),
        "hash_seed": jax.random.randint(seeds[6], (), 0, 1000000).astype(jnp.int32),
        "step_count": jax.random.randint(seeds[7], (), 1, 30).astype(jnp.int32),
    }


def projection(hash_seed, rows_count, cols_count):
    row_ids = lax.broadcasted_iota(jnp.int32, (rows_count, cols_count), 0)
    col_ids = lax.broadcasted_iota(jnp.int32, (rows_count, cols_count), 1)
    mixed = (row_ids * cols_count + col_ids) * jnp.int32(-1640531535) + hash_seed * jnp.int32(668265263)
    mixed = mixed ^ lax.shift_right_logical(mixed, jnp.int32(15))
    mixed = mixed * jnp.int32(-2048144777)
    mixed = mixed ^ lax.shift_right_logical(mixed, jnp.int32(13))
    mixed = mixed * jnp.int32(-1028477379)
    mixed = mixed ^ lax.shift_right_logical(mixed, jnp.int32(16))
    level = (lax.shift_right_logical(mixed, jnp.int32(8)) & jnp.int32(65535)).astype(jnp.float32)
    return ((level + 0.5) * (2.0 / 65536.0) - 1.0) * math.sqrt(3.0 / cols_count)

def reference(inputs, pre_activation, upstream, weight, first_moment, second_moment, hash_seed, step_count):
    pre_value = pre_activation.astype(jnp.float32)
    upstream_value = upstream.astype(jnp.float32)
    sigmoid_value = jax.nn.sigmoid(pre_value)
    grad_pre = (upstream_value * sigmoid_value * (1.0 + pre_value * (1.0 - sigmoid_value))).astype(jnp.bfloat16)
    projector = projection(hash_seed, OUT_CHANNELS, LOW_RANK).astype(jnp.bfloat16)
    proj_grad = jnp.dot(grad_pre.reshape(TOKENS, OUT_CHANNELS), projector, preferred_element_type=jnp.float32)
    proj_grad = proj_grad.astype(jnp.bfloat16).reshape(SAMPLES, FRAMES, HEIGHT, WIDTH, LOW_RANK)
    pad_spec = ((0, 0), (1, 1), (1, 1), (1, 1), (0, 0))
    grad_padded = jnp.pad(grad_pre, pad_spec)
    proj_padded = jnp.pad(proj_grad, pad_spec)
    flat_source = inputs.reshape(TOKENS, IN_CHANNELS)
    branch = jnp.zeros((TOKENS, IN_CHANNELS), jnp.float32)
    terms = []
    for offset in range(27):
        along_t = 2 - offset // 9
        along_h = 2 - offset // 3 % 3
        along_w = 2 - offset % 3
        shifted = grad_padded[:, along_t:along_t + FRAMES, along_h:along_h + HEIGHT, along_w:along_w + WIDTH, :]
        branch = branch + jnp.dot(shifted.reshape(TOKENS, OUT_CHANNELS), weight[offset].T, preferred_element_type=jnp.float32)
        shifted_proj = proj_padded[:, along_t:along_t + FRAMES, along_h:along_h + HEIGHT, along_w:along_w + WIDTH, :]
        terms.append(jnp.dot(flat_source.T, shifted_proj.reshape(TOKENS, LOW_RANK), preferred_element_type=jnp.float32))
    input_grad = (upstream_value.reshape(TOKENS, IN_CHANNELS) + branch).astype(jnp.bfloat16)
    input_grad = input_grad.reshape(SAMPLES, FRAMES, HEIGHT, WIDTH, IN_CHANNELS)
    reduced = jnp.stack(terms, axis=1).reshape(IN_CHANNELS * 27, LOW_RANK) / math.sqrt(TOKENS)
    new_first = 0.9 * first_moment + 0.1 * reduced
    new_second = 0.999 * second_moment + 0.001 * reduced * reduced
    step_value = step_count.astype(jnp.float32)
    first_bias = 1.0 - jnp.power(jnp.float32(0.9), step_value)
    second_bias = 1.0 - jnp.power(jnp.float32(0.999), step_value)
    adapted = new_first / first_bias / (jnp.sqrt(new_second / second_bias) + 1e-08)
    scales = jnp.sqrt(lax.optimization_barrier(jnp.mean(adapted * adapted, axis=1))) / jnp.sqrt(lax.optimization_barrier(jnp.mean(reduced * reduced, axis=1)) + 1e-06)
    return (input_grad, new_first, new_second, scales)
```

```python
import functools
import math

import jax
import jax.numpy as jnp
import ml_dtypes
import numpy as np
from jax import lax
from jax.experimental import pallas as pl
from jax.experimental.pallas import tpu as pltpu
from jax.sharding import PartitionSpec as P

MESH = pl.DeviceIdType.MESH


def extended(cells, sides, width):
    for axis, dim in sides:
        count = lax.axis_size(axis)
        ends = count - 1
        head = lax.slice_in_dim(cells, 0, width, axis=dim)
        tail = lax.slice_in_dim(cells, cells.shape[dim] - width, cells.shape[dim], axis=dim)
        cells = jnp.concatenate(
            [
                lax.ppermute(tail, axis, [(i, (i + 1) % count) for i in range(ends)]),
                cells,
                lax.ppermute(head, axis, [((i + 1) % count, i) for i in range(ends)]),
            ],
            axis=dim,
        )
    return cells


def projection(hash_seed, rows_count, cols_count):
    row_ids = lax.broadcasted_iota(jnp.int32, (rows_count, cols_count), 0)
    col_ids = lax.broadcasted_iota(jnp.int32, (rows_count, cols_count), 1)
    mixed = (row_ids * cols_count + col_ids) * jnp.int32(-1640531535) + hash_seed * jnp.int32(
        668265263
    )
    mixed = mixed ^ lax.shift_right_logical(mixed, jnp.int32(15))
    mixed = mixed * jnp.int32(-2048144777)
    mixed = mixed ^ lax.shift_right_logical(mixed, jnp.int32(13))
    mixed = mixed * jnp.int32(-1028477379)
    mixed = mixed ^ lax.shift_right_logical(mixed, jnp.int32(16))
    level = (lax.shift_right_logical(mixed, jnp.int32(8)) & jnp.int32(65535)).astype(jnp.float32)
    return ((level + 0.5) * (2.0 / 65536.0) - 1.0) * math.sqrt(3.0 / cols_count)


def pad_time(volume):
    return jnp.pad(volume, ((1, 1), (0, 0), (0, 0), (0, 0)))


def windows(padded, stack_axis):
    frame_count = padded.shape[0] - 2
    height_count = padded.shape[1] - 2
    width_count = padded.shape[2] - 2
    channels = padded.shape[3]
    pieces = []
    for offset in range(27):
        along_t = offset // 9
        along_h = offset // 3 % 3
        along_w = offset % 3
        along_t, along_h, along_w = (2 - along_t, 2 - along_h, 2 - along_w)
        window_block = padded[
            along_t : along_t + frame_count,
            along_h : along_h + height_count,
            along_w : along_w + width_count,
        ]
        pieces.append(window_block.reshape(frame_count * height_count * width_count, channels))
    return jnp.stack(pieces, axis=stack_axis)


def update(summed, token_total, first_moment, second_moment, step_count):
    reduced = summed / math.sqrt(token_total)
    new_first = 0.9 * first_moment + 0.1 * reduced
    new_second = 0.999 * second_moment + 0.001 * reduced * reduced
    step_value = step_count.astype(jnp.float32)
    first_bias = 1.0 - jnp.power(jnp.float32(0.9), step_value)
    second_bias = 1.0 - jnp.power(jnp.float32(0.999), step_value)
    adapted = new_first / first_bias / (jnp.sqrt(new_second / second_bias) + 1e-08)
    scales = jnp.sqrt(jnp.mean(adapted * adapted, axis=1)) / jnp.sqrt(
        jnp.mean(reduced * reduced, axis=1) + 1e-06
    )
    return (new_first, new_second, scales)


def body(
    inputs, pre_activation, upstream, weight, first_moment, second_moment, hash_seed, step_count
):
    source = inputs[0]
    frame_count, height_count, width_count, in_width = source.shape
    tokens_here = frame_count * height_count * width_count
    out_width = pre_activation.shape[-1]
    rank_width = first_moment.shape[1]
    rows_here = first_moment.shape[0]
    pre_value = pre_activation[0].astype(jnp.float32)
    upstream_value = upstream[0].astype(jnp.float32)
    sigmoid_value = jax.nn.sigmoid(pre_value)
    grad_pre = (upstream_value * sigmoid_value * (1.0 + pre_value * (1.0 - sigmoid_value))).astype(
        jnp.bfloat16
    )
    projector = projection(hash_seed, out_width, rank_width).astype(jnp.bfloat16)
    proj_grad = jnp.dot(
        grad_pre.reshape(tokens_here, out_width), projector, preferred_element_type=jnp.float32
    )
    proj_grad = proj_grad.astype(jnp.bfloat16)
    joined = jnp.concatenate(
        [grad_pre, proj_grad.reshape(frame_count, height_count, width_count, rank_width)], axis=3
    )
    joined = pad_time(extended(joined, (("sy", 1), ("sx", 2)), 1))
    grad_padded = joined[..., :out_width]
    proj_cols = windows(joined[..., out_width:], 1)
    flat_source = source.reshape(tokens_here, in_width)
    grad_cols = windows(grad_padded, 1)
    branch = jnp.einsum(
        "toc,oic->ti",
        grad_cols,
        lax.all_gather(weight, "dp", axis=1, tiled=True),
        preferred_element_type=jnp.float32,
    )
    input_grad = (upstream_value.reshape(tokens_here, in_width) + branch).astype(jnp.bfloat16)
    input_grad = input_grad.reshape(1, frame_count, height_count, width_count, in_width)
    product = jnp.einsum("tc,tor->cor", flat_source, proj_cols, preferred_element_type=jnp.float32)
    summed = lax.psum_scatter(
        product.reshape(rows_here * lax.axis_size(("dp", "sy", "sx")) // 27 * 27, rank_width),
        ("dp", "sy", "sx"),
        scatter_dimension=0,
        tiled=True,
    )
    token_total = tokens_here * lax.axis_size("dp") * lax.axis_size("sy") * lax.axis_size("sx")
    return (input_grad, *update(summed, token_total, first_moment, second_moment, step_count))


def tables(frames, high, wide, sy_count, sx_count, dp_count, chunk, channels):
    cell = high * wide
    own = frames * cell
    pieces = []
    offset = 0
    for da in (-1, 0, 1):
        for db in (-1, 0, 1):
            if da == 0 and db == 0:
                continue
            rows = [0 if da < 0 else high - 1] if da else list(range(high))
            cols = [0 if db < 0 else wide - 1] if db else list(range(wide))
            spots = [(h, w) for h in rows for w in cols]
            size = -(-frames * len(spots) // 16) * 16
            pieces.append((da, db, spots, offset, size))
            offset += size
    edge = np.zeros((offset, own), np.float32)
    shared = sx_count == 2
    slots = {}
    for h in range(high):
        for w in range(wide):
            slots[(h, w)] = len(slots)
    for da, db, spots, start, _ in pieces:
        for h, w in spots:
            spot = (h if not da else (high if da < 0 else -1), w if not db else (wide if db < 0 else -1))
            other = (spot[0], wide if spot[1] == -1 else -1)
            if shared and db and other in slots:
                slots[spot] = slots[other]
            else:
                slots[spot] = len(set(slots.values()))
    span = -(-len(set(slots.values())) // 16) * 16
    gather_own = np.zeros((frames * span, own), np.float32)
    gather_halo = np.zeros((frames * span, offset), np.float32)
    for t in range(frames):
        for place in range(cell):
            gather_own[t * span + place, t * cell + place] = 1
        for da, db, spots, start, _ in pieces:
            for n, (h, w) in enumerate(spots):
                edge[start + t * len(spots) + n, t * cell + h * wide + w] = 1
                spot = (h if not da else (high if da < 0 else -1), w if not db else (wide if db < 0 else -1))
                gather_halo[t * span + slots[spot], start + t * len(spots) + n] = 1
    select = np.zeros((2, 9 * cell, span), np.float32)
    for side in range(2):
        for j in range(9):
            for h in range(high):
                for w in range(wide):
                    at = (h + 1 - j // 3, w + 1 - j % 3)
                    if shared and at[1] == (-1 if side == 0 else wide):
                        continue
                    select[side, j * cell + h * wide + w, slots[at]] = 1
    peers = sy_count * sx_count
    ids = np.arange(peers * cell)
    peer, inner = ids // cell, ids % cell
    row = peer // sx_count * high + inner // wide
    col = peer % sx_count * wide + inner % wide
    shift = np.zeros((peers * cell, 9 * peers * cell), np.float32)
    for j in range(9):
        hit = (row[:, None] == row[None] + j // 3 - 1) & (col[:, None] == col[None] + j % 3 - 1)
        shift[:, j * peers * cell : (j + 1) * peers * cell] = hit
    group = np.zeros((2, channels, peers * 128), np.float32)
    for part in range(2):
        for d in range(dp_count):
            for p in range(peers):
                for c in range(chunk):
                    group[part, (d * peers + p) * chunk + c, p * 128 + part * 64 + d * 16 + c] = 1
    cast = [m.astype(ml_dtypes.bfloat16) for m in (edge, gather_own, gather_halo, select, shift, group)]
    return pieces, span, cast


def dot(left, right):
    return jnp.dot(left, right, preferred_element_type=jnp.float32)


def kernel(
    sizes, pieces,
    grad_ref, source_ref, upstream_ref, projector_ref, weight_hbm,
    edge_ref, gather_own_ref, gather_halo_ref, select_ref, shift_ref, group_ref,
    out_ref, reduced_ref,
    weight, edges, halo, blocks, windows_buf, packed, packed_in, proj, proj_in,
    shifted, parts, part_out, part_in, total, branch_in,
    weight_sem, halo_send, halo_recv, pack_send, pack_recv, proj_send, proj_recv,
    block_send, block_recv, part_send, part_recv, branch_send, branch_recv,
):
    dp, sy, sx, frames, cell, span = sizes
    peers = sy * sx
    half = frames // 2
    frame = peers * cell
    bf16 = jnp.bfloat16
    d, a, b = lax.axis_index("dp"), lax.axis_index("sy"), lax.axis_index("sx")
    me = a * sx + b

    load = pltpu.make_async_copy(weight_hbm, weight, weight_sem)
    load.start()

    def peer_at(step):
        other = (me + step) % peers
        return other, (d, other // sx, other % sx)

    def dp_at(step):
        other = (d + step) % dp
        return other, (other, a, b)

    barrier = pltpu.get_barrier_semaphore()
    for step in range(1, peers):
        pl.semaphore_signal(barrier, inc=1, device_id=peer_at(step)[1], device_id_type=MESH)
    for step in range(1, dp):
        pl.semaphore_signal(barrier, inc=1, device_id=dp_at(step)[1], device_id_type=MESH)

    edges[...] = dot(edge_ref[...], grad_ref[...]).astype(bf16)
    proj[...] = dot(grad_ref[...], projector_ref[...]).astype(bf16).reshape(proj.shape)
    pl.semaphore_wait(barrier, peers + dp - 2)

    def halo_copy(k):
        da, db, _, start, size = pieces[k]
        to_a = jnp.clip(a + da, 0, sy - 1)
        to_b = jnp.clip(b + db, 0, sx - 1)
        return pltpu.make_async_remote_copy(
            src_ref=edges.at[pl.ds(start, size)], dst_ref=halo.at[pl.ds(start, size)],
            send_sem=halo_send.at[k], recv_sem=halo_recv.at[k],
            device_id=(d, to_a, to_b), device_id_type=MESH,
        )

    def inside(at, count, move):
        return (at + move >= 0) & (at + move < count)

    for k, (da, db, _, start, size) in enumerate(pieces):
        @pl.when(inside(a, sy, da) & inside(b, sx, db))
        def _(k=k):
            halo_copy(k).start()

        @pl.when(jnp.logical_not(inside(a, sy, -da) & inside(b, sx, -db)))
        def _(start=start, size=size):
            halo[pl.ds(start, size), :] = jnp.zeros((size, halo.shape[1]), bf16)

    mine = pl.ds(pl.multiple_of(me * cell, 16), cell)
    proj_copies = []
    for step in range(1, peers):
        proj_copies.append(pltpu.make_async_remote_copy(
            src_ref=proj, dst_ref=proj_in.at[:, mine, :],
            send_sem=proj_send.at[step], recv_sem=proj_recv.at[step],
            device_id=peer_at(step)[1], device_id_type=MESH,
        ))
        proj_copies[-1].start()
    split = half * cell
    spread = dot(source_ref[:split, :], group_ref[0]) + dot(source_ref[split:, :], group_ref[1])
    spread = spread.astype(bf16)
    for p in range(peers):
        packed[p] = spread[:, p * 128 : (p + 1) * 128].reshape(half, cell, 128)
    pack_copies = []
    for step in range(1, peers):
        other, place = peer_at(step)
        pack_copies.append(pltpu.make_async_remote_copy(
            src_ref=packed.at[other], dst_ref=packed_in.at[:, mine, :],
            send_sem=pack_send.at[step], recv_sem=pack_recv.at[step],
            device_id=place, device_id_type=MESH,
        ))
        pack_copies[-1].start()
    packed_in[:, mine, :] = packed[me]
    proj_in[:, mine, :] = proj[...]

    for k, (da, db, _, start, size) in enumerate(pieces):
        @pl.when(inside(a, sy, -da) & inside(b, sx, -db))
        def _(k=k):
            halo_copy(k).wait_recv()

    block = dot(gather_own_ref[...], grad_ref[...]) + dot(gather_halo_ref[...], halo[...])
    blocks[d] = block.astype(bf16).reshape(frames, span, block.shape[1])

    def flip(at, bit):
        return at + bit * (1 - 2 * ((at // bit) % 2))

    block_copies = []
    bits = []
    bit = dp // 2
    while bit:
        bits.append(bit)
        bit //= 2

    def send_block(bit, mask, wait_first):
        if wait_first is not None:
            wait_first.wait_recv()
        slot = d
        for one in bits:
            if mask & one:
                slot = flip(slot, one)
        n = len(block_copies)
        block_copies.append(pltpu.make_async_remote_copy(
            src_ref=blocks.at[slot], dst_ref=blocks.at[slot],
            send_sem=block_send.at[n], recv_sem=block_recv.at[n],
            device_id=(flip(d, bit), a, b), device_id_type=MESH,
        ))
        block_copies[-1].start()
        return block_copies[-1]

    arrivals = {}
    for bit in bits:
        arrivals[bit] = send_block(bit, 0, None)

    for copy in pack_copies + proj_copies:
        copy.wait_recv()

    for ot in (-1, 1):
        last = frames - 1 if ot > 0 else 0
        for c in range(dp):
            shifted[c, pl.ds(9 * (ot + 1), 9), :, pl.ds(last * frame, frame)] = jnp.zeros(
                (9, 16, frame), bf16
            )
    for n in range(half):
        turned = packed_in[n].astype(jnp.float32).T.astype(bf16)
        moved = dot(turned, shift_ref[...]).astype(bf16)
        for j in range(9):
            piece = moved[:, j * frame : (j + 1) * frame]
            for part in range(2):
                for ot in (-1, 0, 1):
                    at = part * half + n - ot
                    if 0 <= at < frames:
                        for c in range(dp):
                            low = part * 64 + c * 16
                            shifted[c, 9 * (ot + 1) + j, :, pl.ds(at * frame, frame)] = piece[
                                low : low + 16
                            ]

    held = [0]
    received = {}
    for bit in bits:
        fresh = []
        for mask in held:
            if mask == 0:
                copy = arrivals[bit]
            else:
                source = received.pop(mask) if mask in received else None
                copy = send_block(bit, mask, source)
            received[mask | bit] = copy
            fresh.append(mask | bit)
        held += fresh

    whole_proj = proj_in[...].reshape(frames * frame, proj_in.shape[2])
    for c in range(dp):
        part = dot(shifted[c].reshape(27 * 16, frames * frame), whole_proj)
        parts[c] = part
        part_out[c] = part.astype(bf16)
    part_copies = []
    for step in range(1, dp):
        other, place = dp_at(step)
        part_copies.append(pltpu.make_async_remote_copy(
            src_ref=part_out.at[other], dst_ref=part_in.at[step],
            send_sem=part_send.at[step], recv_sem=part_recv.at[step],
            device_id=place, device_id_type=MESH,
        ))
        part_copies[-1].start()

    for copy in received.values():
        copy.wait_recv()
    depth = windows_buf.shape[-1]
    edge_zero = jnp.zeros((9, dp, cell, depth), bf16)
    windows_buf[:, :, 0] = edge_zero
    windows_buf[:, :, frames + 1] = edge_zero

    def build(n, carry):
        s, t = n // frames, n % frames
        found = dot(select_ref[...], blocks[s, t]).astype(bf16)
        windows_buf[:, s, t + 1] = found.reshape(9, cell, depth)
        return carry

    lax.fori_loop(0, dp * frames, build, 0)
    load.wait()
    total[...] = jnp.zeros(total.shape, jnp.float32)

    def tap_step(j, carry):
        value = total[...]
        for t in range(3):
            rows = windows_buf[j, :, 2 - t : 2 - t + frames].reshape(dp * frames * cell, depth)
            value = value + lax.dot_general(
                rows, weight[t * 9 + j], (((1,), (1,)), ((), ())),
                preferred_element_type=jnp.float32,
            )
        total[...] = value
        return carry

    lax.fori_loop(0, 9, tap_step, 0)
    tokens = frames * cell
    branch_copies = []
    for step in range(1, dp):
        other, place = dp_at(step)
        branch_copies.append(pltpu.make_async_remote_copy(
            src_ref=total.at[pl.ds(pl.multiple_of(other * tokens, 16), tokens)],
            dst_ref=branch_in.at[d],
            send_sem=branch_send.at[step], recv_sem=branch_recv.at[step],
            device_id=place, device_id_type=MESH,
        ))
        branch_copies[-1].start()
    branch_in[d] = total[pl.ds(pl.multiple_of(d * tokens, 16), tokens), :]

    for copy in part_copies:
        copy.wait_recv()
    summed = parts[d]
    for step in range(1, dp):
        summed = summed + part_in[step].astype(jnp.float32)
    reduced_ref[...] = summed
    for copy in branch_copies:
        copy.wait_recv()
    width = branch_in.shape[2]
    for c in range(dp):
        cols = slice(c * width, (c + 1) * width)
        out_ref[:, cols] = (upstream_ref[:, cols].astype(jnp.float32) + branch_in[c]).astype(bf16)

    for k, (da, db, _, start, size) in enumerate(pieces):
        @pl.when(inside(a, sy, da) & inside(b, sx, db))
        def _(k=k):
            halo_copy(k).wait_send()
    for copy in proj_copies + pack_copies + block_copies + part_copies + branch_copies:
        copy.wait_send()


def fused_body(
    inputs, pre_activation, upstream, weight, first_moment, second_moment, hash_seed, step_count
):
    source = inputs[0]
    frames, high, wide, channels = source.shape
    depth = pre_activation.shape[-1]
    rank = first_moment.shape[1]
    dp, sy, sx = (lax.axis_size(name) for name in ("dp", "sy", "sx"))
    cell, peers = high * wide, sy * sx
    tokens, frame = frames * cell, peers * cell
    chunk = first_moment.shape[0] // 27
    ci = weight.shape[1]
    pieces, span, consts = tables(frames, high, wide, sy, sx, dp, chunk, channels)
    edge, gather_own, gather_halo, select, shift, group = consts
    side = (lax.axis_index("sx") > 0).astype(jnp.int32)
    select = lax.dynamic_index_in_dim(jnp.asarray(select), side, 0, keepdims=False)
    pre_value = pre_activation[0].astype(jnp.float32)
    upstream_value = upstream[0].astype(jnp.float32)
    sigmoid_value = jax.nn.sigmoid(pre_value)
    grad_pre = (upstream_value * sigmoid_value * (1.0 + pre_value * (1.0 - sigmoid_value))).astype(
        jnp.bfloat16
    )
    projector = projection(hash_seed, depth, rank).astype(jnp.bfloat16)
    halo_rows = edge.shape[0]
    bf16, f32 = jnp.bfloat16, jnp.float32
    dma = pltpu.SemaphoreType.DMA
    vmem = pl.BlockSpec(memory_space=pltpu.VMEM)
    input_grad, summed = pl.pallas_call(
        functools.partial(kernel, (dp, sy, sx, frames, cell, span), pieces),
        out_shape=(
            jax.ShapeDtypeStruct((tokens, channels), bf16),
            jax.ShapeDtypeStruct((27 * 16, rank), f32),
        ),
        in_specs=[vmem] * 4 + [pl.BlockSpec(memory_space=pl.ANY)] + [vmem] * 6,
        out_specs=(vmem, vmem),
        scratch_shapes=[
            pltpu.VMEM(weight.shape, bf16),
            pltpu.VMEM((halo_rows, depth), bf16),
            pltpu.VMEM((halo_rows, depth), bf16),
            pltpu.VMEM((dp, frames, span, depth), bf16),
            pltpu.VMEM((9, dp, frames + 2, cell, depth), bf16),
            pltpu.VMEM((peers, frames // 2, cell, 128), bf16),
            pltpu.VMEM((frames // 2, frame, 128), bf16),
            pltpu.VMEM((frames, cell, rank), bf16),
            pltpu.VMEM((frames, frame, rank), bf16),
            pltpu.VMEM((dp, 27, 16, frames * frame), bf16),
            pltpu.VMEM((dp, 27 * 16, rank), f32),
            pltpu.VMEM((dp, 27 * 16, rank), bf16),
            pltpu.VMEM((dp, 27 * 16, rank), bf16),
            pltpu.VMEM((dp * tokens, ci), f32),
            pltpu.VMEM((dp, tokens, ci), f32),
            dma,
            dma((8,)), dma((8,)),
            dma((peers,)), dma((peers,)),
            dma((peers,)), dma((peers,)),
            dma((dp,)), dma((dp,)),
            dma((dp,)), dma((dp,)),
            dma((dp,)), dma((dp,)),
        ],
        compiler_params=pltpu.CompilerParams(
            collective_id=0, has_side_effects=True, vmem_limit_bytes=48 * 1024 * 1024
        ),
    )(
        grad_pre.reshape(tokens, depth),
        source.reshape(tokens, channels),
        upstream[0].reshape(tokens, channels),
        projector,
        weight,
        jnp.asarray(edge), jnp.asarray(gather_own), jnp.asarray(gather_halo), select,
        jnp.asarray(shift), jnp.asarray(group),
    )
    input_grad = input_grad.reshape(1, frames, high, wide, channels)
    summed = summed.reshape(27, 16, rank)[:, :chunk].transpose(1, 0, 2).reshape(27 * chunk, rank)
    return (input_grad, *update(summed, tokens * dp * peers, first_moment, second_moment, step_count))


def fits(mesh, args):
    dp, sy, sx = mesh.shape["dp"], mesh.shape["sy"], mesh.shape["sx"]
    _, frames, high, wide, channels = args[0].shape
    rank = args[4].shape[1]
    high, wide, peers = high // sy, wide // sx, sy * sx
    cell = high * wide
    frame = cell * peers
    chunk = args[4].shape[0] // 27 // (dp * peers)
    depth = args[3].shape[2]
    return (
        dp == 4
        and args[0].shape[0] == dp
        and frames % 2 == 0
        and cell % 16 == 0
        and frame % 128 == 0
        and chunk <= 16
        and rank % 128 == 0
        and channels % (128 * dp) == 0
        and depth % 128 == 0
        and 18 * frame * frame + 512 * channels * peers < 6 * 2**20
        and 2 * 27 * (64 * frames * frame + channels // dp * depth) < 16 * 2**20
        and 18 * dp * (frames + 2) * cell * depth < 12 * 2**20
    )


def solution(mesh):
    placed = (
        P("dp", None, "sy", "sx", None),
        P("dp", None, "sy", "sx", None),
        P("dp", None, "sy", "sx", None),
        P(None, "dp", None),
        P(("dp", "sy", "sx"), None),
        P(("dp", "sy", "sx"), None),
        P(),
        P(),
    )
    def run(*args):
        return mapped(fused_body if fits(mesh, args) else body)(*args)

    def mapped(part):
      return jax.shard_map(
        part,
        mesh=mesh,
        in_specs=placed,
        out_specs=(
            P("dp", None, "sy", "sx", None),
            P(("dp", "sy", "sx"), None),
            P(("dp", "sy", "sx"), None),
            P(("dp", "sy", "sx")),
        ),
        check_vma=False,
    )

    return run
```

```python
import functools
import math

import jax
import jax.numpy as jnp
import ml_dtypes
import numpy as np
from jax import lax
from jax.experimental import pallas as pl
from jax.experimental.pallas import tpu as pltpu
from jax.sharding import PartitionSpec as P

MESH = pl.DeviceIdType.MESH


def extended(cells, sides, width):
    for axis, dim in sides:
        count = lax.axis_size(axis)
        ends = count - 1
        head = lax.slice_in_dim(cells, 0, width, axis=dim)
        tail = lax.slice_in_dim(cells, cells.shape[dim] - width, cells.shape[dim], axis=dim)
        cells = jnp.concatenate(
            [
                lax.ppermute(tail, axis, [(i, (i + 1) % count) for i in range(ends)]),
                cells,
                lax.ppermute(head, axis, [((i + 1) % count, i) for i in range(ends)]),
            ],
            axis=dim,
        )
    return cells


def projection(hash_seed, rows_count, cols_count):
    row_ids = lax.broadcasted_iota(jnp.int32, (rows_count, cols_count), 0)
    col_ids = lax.broadcasted_iota(jnp.int32, (rows_count, cols_count), 1)
    mixed = (row_ids * cols_count + col_ids) * jnp.int32(-1640531535) + hash_seed * jnp.int32(
        668265263
    )
    mixed = mixed ^ lax.shift_right_logical(mixed, jnp.int32(15))
    mixed = mixed * jnp.int32(-2048144777)
    mixed = mixed ^ lax.shift_right_logical(mixed, jnp.int32(13))
    mixed = mixed * jnp.int32(-1028477379)
    mixed = mixed ^ lax.shift_right_logical(mixed, jnp.int32(16))
    level = (lax.shift_right_logical(mixed, jnp.int32(8)) & jnp.int32(65535)).astype(jnp.float32)
    return ((level + 0.5) * (2.0 / 65536.0) - 1.0) * math.sqrt(3.0 / cols_count)


def pad_time(volume):
    return jnp.pad(volume, ((1, 1), (0, 0), (0, 0), (0, 0)))


def windows(padded, stack_axis):
    frame_count = padded.shape[0] - 2
    height_count = padded.shape[1] - 2
    width_count = padded.shape[2] - 2
    channels = padded.shape[3]
    pieces = []
    for offset in range(27):
        along_t = offset // 9
        along_h = offset // 3 % 3
        along_w = offset % 3
        along_t, along_h, along_w = (2 - along_t, 2 - along_h, 2 - along_w)
        window_block = padded[
            along_t : along_t + frame_count,
            along_h : along_h + height_count,
            along_w : along_w + width_count,
        ]
        pieces.append(window_block.reshape(frame_count * height_count * width_count, channels))
    return jnp.stack(pieces, axis=stack_axis)


def update(summed, token_total, first_moment, second_moment, step_count):
    reduced = summed / math.sqrt(token_total)
    new_first = 0.9 * first_moment + 0.1 * reduced
    new_second = 0.999 * second_moment + 0.001 * reduced * reduced
    step_value = step_count.astype(jnp.float32)
    first_bias = 1.0 - jnp.power(jnp.float32(0.9), step_value)
    second_bias = 1.0 - jnp.power(jnp.float32(0.999), step_value)
    adapted = new_first / first_bias / (jnp.sqrt(new_second / second_bias) + 1e-08)
    scales = jnp.sqrt(jnp.mean(adapted * adapted, axis=1)) / jnp.sqrt(
        jnp.mean(reduced * reduced, axis=1) + 1e-06
    )
    return (new_first, new_second, scales)


def body(
    inputs, pre_activation, upstream, weight, first_moment, second_moment, hash_seed, step_count
):
    source = inputs[0]
    frame_count, height_count, width_count, in_width = source.shape
    tokens_here = frame_count * height_count * width_count
    out_width = pre_activation.shape[-1]
    rank_width = first_moment.shape[1]
    rows_here = first_moment.shape[0]
    pre_value = pre_activation[0].astype(jnp.float32)
    upstream_value = upstream[0].astype(jnp.float32)
    sigmoid_value = jax.nn.sigmoid(pre_value)
    grad_pre = (upstream_value * sigmoid_value * (1.0 + pre_value * (1.0 - sigmoid_value))).astype(
        jnp.bfloat16
    )
    projector = projection(hash_seed, out_width, rank_width).astype(jnp.bfloat16)
    proj_grad = jnp.dot(
        grad_pre.reshape(tokens_here, out_width), projector, preferred_element_type=jnp.float32
    )
    proj_grad = proj_grad.astype(jnp.bfloat16)
    joined = jnp.concatenate(
        [grad_pre, proj_grad.reshape(frame_count, height_count, width_count, rank_width)], axis=3
    )
    joined = pad_time(extended(joined, (("sy", 1), ("sx", 2)), 1))
    grad_padded = joined[..., :out_width]
    proj_cols = windows(joined[..., out_width:], 1)
    flat_source = source.reshape(tokens_here, in_width)
    grad_cols = windows(grad_padded, 1)
    branch = jnp.einsum(
        "toc,oic->ti",
        grad_cols,
        lax.all_gather(weight, "dp", axis=1, tiled=True),
        preferred_element_type=jnp.float32,
    )
    input_grad = (upstream_value.reshape(tokens_here, in_width) + branch).astype(jnp.bfloat16)
    input_grad = input_grad.reshape(1, frame_count, height_count, width_count, in_width)
    product = jnp.einsum("tc,tor->cor", flat_source, proj_cols, preferred_element_type=jnp.float32)
    summed = lax.psum_scatter(
        product.reshape(rows_here * lax.axis_size(("dp", "sy", "sx")) // 27 * 27, rank_width),
        ("dp", "sy", "sx"),
        scatter_dimension=0,
        tiled=True,
    )
    token_total = tokens_here * lax.axis_size("dp") * lax.axis_size("sy") * lax.axis_size("sx")
    return (input_grad, *update(summed, token_total, first_moment, second_moment, step_count))


def tables(frames, high, wide, sy_count, sx_count, dp_count, chunk, channels):
    cell = high * wide
    own = frames * cell
    pieces = []
    offset = 0
    for da in (-1, 0, 1):
        for db in (-1, 0, 1):
            if da == 0 and db == 0:
                continue
            rows = [0 if da < 0 else high - 1] if da else list(range(high))
            cols = [0 if db < 0 else wide - 1] if db else list(range(wide))
            spots = [(h, w) for h in rows for w in cols]
            size = -(-frames * len(spots) // 16) * 16
            pieces.append((da, db, spots, offset, size))
            offset += size
    edge = np.zeros((offset, own), np.float32)
    shared = sx_count == 2
    slots = {}
    for h in range(high):
        for w in range(wide):
            slots[(h, w)] = len(slots)
    for da, db, spots, start, _ in pieces:
        for h, w in spots:
            spot = (h if not da else (high if da < 0 else -1), w if not db else (wide if db < 0 else -1))
            other = (spot[0], wide if spot[1] == -1 else -1)
            if shared and db and other in slots:
                slots[spot] = slots[other]
            else:
                slots[spot] = len(set(slots.values()))
    span = -(-len(set(slots.values())) // 16) * 16
    gather_own = np.zeros((frames * span, own), np.float32)
    gather_halo = np.zeros((frames * span, offset), np.float32)
    for t in range(frames):
        for place in range(cell):
            gather_own[t * span + place, t * cell + place] = 1
        for da, db, spots, start, _ in pieces:
            for n, (h, w) in enumerate(spots):
                edge[start + t * len(spots) + n, t * cell + h * wide + w] = 1
                spot = (h if not da else (high if da < 0 else -1), w if not db else (wide if db < 0 else -1))
                gather_halo[t * span + slots[spot], start + t * len(spots) + n] = 1
    select = np.zeros((2, 9, frames, cell, frames, span), np.float32)
    for side in range(2):
        for j in range(9):
            for h in range(high):
                for w in range(wide):
                    at = (h + 1 - j // 3, w + 1 - j % 3)
                    if shared and at[1] == (-1 if side == 0 else wide):
                        continue
                    for t in range(frames):
                        select[side, j, t, h * wide + w, t, slots[at]] = 1
    select = select.reshape(2, 9 * frames * cell, frames * span)
    order = np.zeros((chunk * 27, 27 * 16), np.float32)
    for c in range(chunk):
        for tap in range(27):
            order[c * 27 + tap, tap * 16 + c] = 1
    peers = sy_count * sx_count
    ids = np.arange(peers * cell)
    peer, inner = ids // cell, ids % cell
    row = peer // sx_count * high + inner // wide
    col = peer % sx_count * wide + inner % wide
    shift = np.zeros((peers * cell, 9 * peers * cell), np.float32)
    for j in range(9):
        hit = (row[:, None] == row[None] + j // 3 - 1) & (col[:, None] == col[None] + j % 3 - 1)
        shift[:, j * peers * cell : (j + 1) * peers * cell] = hit
    group = np.zeros((2, channels, peers * 128), np.float32)
    for part in range(2):
        for d in range(dp_count):
            for p in range(peers):
                for c in range(chunk):
                    group[part, (d * peers + p) * chunk + c, p * 128 + part * 64 + d * 16 + c] = 1
    cast = [m.astype(ml_dtypes.bfloat16) for m in (edge, gather_own, gather_halo, select, shift, group, order)]
    return pieces, span, cast


def dot(left, right):
    return jnp.dot(left, right, preferred_element_type=jnp.float32)


def kernel(
    sizes, pieces,
    pre_ref, source_in, upstream_in, projector_ref, bias_ref, weight_hbm, first_hbm, second_hbm,
    edge_hbm, own_hbm, halo_hbm, select_hbm, shift_hbm, group_hbm, order_hbm,
    out_ref, first_out, second_out, scales_out,
    grad_ref, source_ref, upstream_ref,
    weight, first, second, edge_ref, gather_own_ref, gather_halo_ref, select_ref, shift_ref,
    group_ref, order_ref,
    edges, halo, blocks, windows_buf, packed, packed_in, proj, proj_in,
    shifted, parts, part_out, part_in, total, branch_in,
    load_sem, halo_send, halo_recv, pack_send, pack_recv, proj_send, proj_recv,
    block_send, block_recv, part_send, part_recv, branch_send, branch_recv,
):
    dp, sy, sx, frames, cell, span = sizes
    peers = sy * sx
    half = frames // 2
    frame = peers * cell
    bf16 = jnp.bfloat16
    d, a, b = lax.axis_index("dp"), lax.axis_index("sy"), lax.axis_index("sx")
    me = a * sx + b

    side = jnp.minimum(b, 1)
    loads = [
        pltpu.make_async_copy(source, target, load_sem.at[n])
        for n, (source, target) in enumerate(
            (
                (edge_hbm, edge_ref),
                (group_hbm, group_ref),
                (own_hbm, gather_own_ref),
                (halo_hbm, gather_halo_ref),
                (shift_hbm, shift_ref),
                (select_hbm.at[side], select_ref),
                (weight_hbm, weight),
                (order_hbm, order_ref),
                (first_hbm, first),
                (second_hbm, second),
            )
        )
    ]
    for load in loads:
        load.start()

    def peer_at(step):
        other = (me + step) % peers
        return other, (d, other // sx, other % sx)

    def dp_at(step):
        other = (d + step) % dp
        return other, (other, a, b)

    barrier = pltpu.get_barrier_semaphore()
    for step in range(1, peers):
        pl.semaphore_signal(barrier, inc=1, device_id=peer_at(step)[1], device_id_type=MESH)
    for step in range(1, dp):
        pl.semaphore_signal(barrier, inc=1, device_id=dp_at(step)[1], device_id_type=MESH)

    wide_shape = upstream_ref.shape
    upstream_value = upstream_in[...].astype(jnp.float32).reshape(wide_shape)
    upstream_ref[...] = upstream_value
    pre_value = pre_ref[...].astype(jnp.float32).reshape(wide_shape)
    sigmoid_value = jax.nn.sigmoid(pre_value)
    grad_ref[...] = (
        upstream_value * sigmoid_value * (1.0 + pre_value * (1.0 - sigmoid_value))
    ).astype(bf16)
    proj[...] = dot(grad_ref[...], projector_ref[...]).astype(bf16).reshape(proj.shape)
    loads[0].wait()
    edges[...] = dot(edge_ref[...], grad_ref[...]).astype(bf16)
    pl.semaphore_wait(barrier, peers + dp - 2)

    def halo_copy(k):
        da, db, _, start, size = pieces[k]
        to_a = jnp.clip(a + da, 0, sy - 1)
        to_b = jnp.clip(b + db, 0, sx - 1)
        return pltpu.make_async_remote_copy(
            src_ref=edges.at[pl.ds(start, size)], dst_ref=halo.at[pl.ds(start, size)],
            send_sem=halo_send.at[k], recv_sem=halo_recv.at[k],
            device_id=(d, to_a, to_b), device_id_type=MESH,
        )

    def inside(at, count, move):
        return (at + move >= 0) & (at + move < count)

    for k, (da, db, _, start, size) in enumerate(pieces):
        @pl.when(inside(a, sy, da) & inside(b, sx, db))
        def _(k=k):
            halo_copy(k).start()

        @pl.when(jnp.logical_not(inside(a, sy, -da) & inside(b, sx, -db)))
        def _(start=start, size=size):
            halo[pl.ds(start, size), :] = jnp.zeros((size, halo.shape[1]), bf16)

    mine = pl.ds(pl.multiple_of(me * cell, 16), cell)
    proj_copies = []
    for step in range(1, peers):
        proj_copies.append(pltpu.make_async_remote_copy(
            src_ref=proj, dst_ref=proj_in.at[:, mine, :],
            send_sem=proj_send.at[step], recv_sem=proj_recv.at[step],
            device_id=peer_at(step)[1], device_id_type=MESH,
        ))
        proj_copies[-1].start()
    source_ref[...] = source_in[...].astype(jnp.float32).reshape(source_ref.shape).astype(bf16)
    loads[1].wait()
    split = half * cell
    spread = dot(source_ref[:split, :], group_ref[0]) + dot(source_ref[split:, :], group_ref[1])
    spread = spread.astype(bf16)
    for p in range(peers):
        packed[p] = spread[:, p * 128 : (p + 1) * 128].reshape(half, cell, 128)
    pack_copies = []
    for step in range(1, peers):
        other, place = peer_at(step)
        pack_copies.append(pltpu.make_async_remote_copy(
            src_ref=packed.at[other], dst_ref=packed_in.at[:, mine, :],
            send_sem=pack_send.at[step], recv_sem=pack_recv.at[step],
            device_id=place, device_id_type=MESH,
        ))
        pack_copies[-1].start()
    packed_in[:, mine, :] = packed[me]
    proj_in[:, mine, :] = proj[...]

    for k, (da, db, _, start, size) in enumerate(pieces):
        @pl.when(inside(a, sy, -da) & inside(b, sx, -db))
        def _(k=k):
            halo_copy(k).wait_recv()

    loads[2].wait()
    loads[3].wait()
    block = dot(gather_own_ref[...], grad_ref[...]) + dot(gather_halo_ref[...], halo[...])
    blocks[d] = block.astype(bf16).reshape(frames, span, block.shape[1])

    def flip(at, bit):
        return at + bit * (1 - 2 * ((at // bit) % 2))

    def masked(mask):
        at = d
        for one in (2, 1):
            if mask & one:
                at = flip(at, one)
        return at

    block_copies = []
    def send_block(bit, mask, wait_first):
        if wait_first is not None:
            wait_first.wait_recv()
        slot = masked(mask)
        n = len(block_copies)
        block_copies.append(pltpu.make_async_remote_copy(
            src_ref=blocks.at[slot], dst_ref=blocks.at[slot],
            send_sem=block_send.at[n], recv_sem=block_recv.at[n],
            device_id=(flip(d, bit), a, b), device_id_type=MESH,
        ))
        block_copies[-1].start()
        return block_copies[-1]

    arrivals = {}
    for bit in (2, 1):
        arrivals[bit] = send_block(bit, 0, None)

    for copy in pack_copies + proj_copies:
        copy.wait_recv()

    for ot in (-1, 1):
        last = frames - 1 if ot > 0 else 0
        for c in range(dp):
            shifted[c, pl.ds(9 * (ot + 1), 9), :, pl.ds(last * frame, frame)] = jnp.zeros(
                (9, 16, frame), bf16
            )
    loads[4].wait()
    for n in range(half):
        turned = packed_in[n].astype(jnp.float32).T.astype(bf16)
        moved = dot(turned, shift_ref[...]).astype(bf16)
        for j in range(9):
            piece = moved[:, j * frame : (j + 1) * frame]
            for part in range(2):
                for ot in (-1, 0, 1):
                    at = part * half + n - ot
                    if 0 <= at < frames:
                        for c in range(dp):
                            low = part * 64 + c * 16
                            shifted[c, 9 * (ot + 1) + j, :, pl.ds(at * frame, frame)] = piece[
                                low : low + 16
                            ]

    whole_proj = proj_in[...].reshape(frames * frame, proj_in.shape[2])
    for c in range(dp):
        part = dot(shifted[c].reshape(27 * 16, frames * frame), whole_proj)
        parts[c] = part
        part_out[c] = part.astype(bf16)
    part_copies = []
    for step in range(1, dp):
        other, place = dp_at(step)
        part_copies.append(pltpu.make_async_remote_copy(
            src_ref=part_out.at[other], dst_ref=part_in.at[step],
            send_sem=part_send.at[step], recv_sem=part_recv.at[step],
            device_id=place, device_id_type=MESH,
        ))
        part_copies[-1].start()

    depth = windows_buf.shape[-1]
    tokens = frames * cell
    loads[5].wait()
    edge_zero = jnp.zeros((9, dp, cell, depth), bf16)
    windows_buf[:, :, 0] = edge_zero
    windows_buf[:, :, frames + 1] = edge_zero

    def build(mask):
        rows = blocks[masked(mask)].reshape(frames * span, depth)
        found = dot(select_ref[...], rows).astype(bf16)
        windows_buf[:, mask, 1 : frames + 1] = found.reshape(9, frames, cell, depth)

    def convolve(mask):
        pair = slice(mask, mask + 2)
        total[pair] = jnp.zeros((2, tokens, total.shape[2]), jnp.float32)

        def tap_step(j, carry):
            value = total[pair].reshape(2 * tokens, total.shape[2])
            for t in range(3):
                rows = windows_buf[j, pair, 2 - t : 2 - t + frames].reshape(2 * tokens, depth)
                value = value + lax.dot_general(
                    rows, weight[t * 9 + j], (((1,), (1,)), ((), ())),
                    preferred_element_type=jnp.float32,
                )
            total[pair] = value.reshape(2, tokens, total.shape[2])
            return carry

        lax.fori_loop(0, 9, tap_step, 0)

    branch_copies = []

    def send_branch(mask):
        branch_copies.append(pltpu.make_async_remote_copy(
            src_ref=total.at[mask], dst_ref=branch_in.at[d],
            send_sem=branch_send.at[mask], recv_sem=branch_recv.at[mask],
            device_id=(masked(mask), a, b), device_id_type=MESH,
        ))
        branch_copies[-1].start()

    build(0)
    arrivals[1].wait_recv()
    build(1)
    onward = send_block(1, 2, arrivals[2])
    loads[6].wait()
    convolve(0)
    send_branch(1)
    build(2)
    onward.wait_recv()
    build(3)
    convolve(2)
    send_branch(3)
    send_branch(2)
    branch_in[d] = total[0]

    for load in loads[7:]:
        load.wait()
    for copy in part_copies:
        copy.wait_recv()
    summed = parts[d]
    for step in range(1, dp):
        summed = summed + part_in[step].astype(jnp.float32)
    ordered = 0.0
    for _ in range(3):
        piece = summed.astype(bf16)
        summed = summed - piece.astype(jnp.float32)
        ordered = ordered + dot(order_ref[...], piece)
    reduced = ordered / math.sqrt(tokens * dp * peers)
    new_first = 0.9 * first[...] + 0.1 * reduced
    new_second = 0.999 * second[...] + 0.001 * reduced * reduced
    first_out[...] = new_first
    second_out[...] = new_second
    adapted = new_first / bias_ref[0] / (jnp.sqrt(new_second / bias_ref[1]) + 1e-08)
    scales_out[...] = jnp.sqrt(jnp.mean(adapted * adapted, axis=1, keepdims=True)) / jnp.sqrt(
        jnp.mean(reduced * reduced, axis=1, keepdims=True) + 1e-06
    )
    for copy in branch_copies:
        copy.wait_recv()
    width = branch_in.shape[2]
    for c in range(dp):
        cols = slice(c * width, (c + 1) * width)
        value = upstream_ref[:, cols] + branch_in[c]
        out_ref[:, :, cols] = value.reshape(*out_ref.shape[:2], width).astype(bf16)

    for k, (da, db, _, start, size) in enumerate(pieces):
        @pl.when(inside(a, sy, da) & inside(b, sx, db))
        def _(k=k):
            halo_copy(k).wait_send()
    for copy in proj_copies + pack_copies + block_copies + part_copies + branch_copies:
        copy.wait_send()


def fused_body(
    inputs, pre_activation, upstream, weight, first_moment, second_moment, hash_seed, step_count
):
    source = inputs[0]
    frames, high, wide, channels = source.shape
    depth = pre_activation.shape[-1]
    rank = first_moment.shape[1]
    dp, sy, sx = (lax.axis_size(name) for name in ("dp", "sy", "sx"))
    cell, peers = high * wide, sy * sx
    tokens, frame = frames * cell, peers * cell
    chunk = first_moment.shape[0] // 27
    ci = weight.shape[1]
    pieces, span, consts = tables(frames, high, wide, sy, sx, dp, chunk, channels)
    edge, gather_own, gather_halo, select, shift, group, order = consts
    step_value = step_count.astype(jnp.float32)
    biases = 1.0 - jnp.power(jnp.asarray([0.9, 0.999], jnp.float32), step_value)
    projector = projection(hash_seed, depth, rank).astype(jnp.bfloat16)
    halo_rows = edge.shape[0]
    bf16, f32 = jnp.bfloat16, jnp.float32
    dma = pltpu.SemaphoreType.DMA
    vmem = pl.BlockSpec(memory_space=pltpu.VMEM)
    hbm = pl.BlockSpec(memory_space=pl.ANY)
    input_grad, new_first, new_second, scales = pl.pallas_call(
        functools.partial(kernel, (dp, sy, sx, frames, cell, span), pieces),
        out_shape=(
            jax.ShapeDtypeStruct((frames * high, wide, channels), bf16),
            jax.ShapeDtypeStruct(first_moment.shape, f32),
            jax.ShapeDtypeStruct(first_moment.shape, f32),
            jax.ShapeDtypeStruct((first_moment.shape[0], 1), f32),
        ),
        in_specs=[vmem] * 4 + [pl.BlockSpec(memory_space=pltpu.SMEM)] + [hbm] * 10,
        out_specs=(vmem,) * 4,
        scratch_shapes=[
            pltpu.VMEM((tokens, depth), bf16),
            pltpu.VMEM((tokens, channels), bf16),
            pltpu.VMEM((tokens, channels), f32),
            pltpu.VMEM(weight.shape, bf16),
            pltpu.VMEM(first_moment.shape, f32),
            pltpu.VMEM(first_moment.shape, f32),
            pltpu.VMEM(edge.shape, bf16),
            pltpu.VMEM(gather_own.shape, bf16),
            pltpu.VMEM(gather_halo.shape, bf16),
            pltpu.VMEM(select.shape[1:], bf16),
            pltpu.VMEM(shift.shape, bf16),
            pltpu.VMEM(group.shape, bf16),
            pltpu.VMEM(order.shape, bf16),
            pltpu.VMEM((halo_rows, depth), bf16),
            pltpu.VMEM((halo_rows, depth), bf16),
            pltpu.VMEM((dp, frames, span, depth), bf16),
            pltpu.VMEM((9, dp, frames + 2, cell, depth), bf16),
            pltpu.VMEM((peers, frames // 2, cell, 128), bf16),
            pltpu.VMEM((frames // 2, frame, 128), bf16),
            pltpu.VMEM((frames, cell, rank), bf16),
            pltpu.VMEM((frames, frame, rank), bf16),
            pltpu.VMEM((dp, 27, 16, frames * frame), bf16),
            pltpu.VMEM((dp, 27 * 16, rank), f32),
            pltpu.VMEM((dp, 27 * 16, rank), bf16),
            pltpu.VMEM((dp, 27 * 16, rank), bf16),
            pltpu.VMEM((dp, tokens, ci), f32),
            pltpu.VMEM((dp, tokens, ci), f32),
            dma((10,)),
            dma((8,)), dma((8,)),
            dma((peers,)), dma((peers,)),
            dma((peers,)), dma((peers,)),
            dma((dp,)), dma((dp,)),
            dma((dp,)), dma((dp,)),
            dma((dp,)), dma((dp,)),
        ],
        compiler_params=pltpu.CompilerParams(
            collective_id=0, has_side_effects=True, vmem_limit_bytes=48 * 1024 * 1024
        ),
    )(
        pre_activation[0].reshape(frames * high, wide, depth),
        source.reshape(frames * high, wide, channels),
        upstream[0].reshape(frames * high, wide, channels),
        projector,
        biases,
        weight,
        first_moment,
        second_moment,
        *(jnp.asarray(m) for m in consts),
    )
    input_grad = input_grad.reshape(1, frames, high, wide, channels)
    return input_grad, new_first, new_second, scales.reshape(first_moment.shape[0])


def fits(mesh, args):
    dp, sy, sx = mesh.shape["dp"], mesh.shape["sy"], mesh.shape["sx"]
    _, frames, high, wide, channels = args[0].shape
    rank = args[4].shape[1]
    high, wide, peers = high // sy, wide // sx, sy * sx
    cell = high * wide
    frame = cell * peers
    chunk = args[4].shape[0] // 27 // (dp * peers)
    depth = args[3].shape[2]
    return (
        dp == 4
        and args[0].shape[0] == dp
        and frames % 2 == 0
        and cell % 16 == 0
        and high * frames % 8 == 0
        and frame % 128 == 0
        and chunk <= 16
        and rank % 128 == 0
        and channels % (128 * dp) == 0
        and depth % 128 == 0
        and 18 * frame * frame + 512 * channels * peers < 6 * 2**20
        and 2 * 27 * (64 * frames * frame + channels // dp * depth) < 16 * 2**20
        and 18 * dp * (frames + 2) * cell * depth < 12 * 2**20
    )


def solution(mesh):
    placed = (
        P("dp", None, "sy", "sx", None),
        P("dp", None, "sy", "sx", None),
        P("dp", None, "sy", "sx", None),
        P(None, "dp", None),
        P(("dp", "sy", "sx"), None),
        P(("dp", "sy", "sx"), None),
        P(),
        P(),
    )
    def run(*args):
        return mapped(fused_body if fits(mesh, args) else body)(*args)

    def mapped(part):
        return jax.shard_map(
        part,
        mesh=mesh,
        in_specs=placed,
        out_specs=(
            P("dp", None, "sy", "sx", None),
            P(("dp", "sy", "sx"), None),
            P(("dp", "sy", "sx"), None),
            P(("dp", "sy", "sx")),
        ),
        check_vma=False,
    )

    return run
```
